32 devices in a mesh: groups: 2 (over y), dom: 4 (over z), feat: 2 (over x), sub: 2 (over core).
Axes of the slice: x: 2, y: 2, z: 4, core: 2. Of those that a mesh axis runs over, the one named last changes fastest.
Arguments:
- grid_lat: bfloat16 [16384, 512], P(('groups', 'dom', 'feat', 'sub')), parts along dimension 0, may hold values from -6 to 6
- mesh_lat: bfloat16 [8192, 512], P(('groups', 'dom', 'feat', 'sub')), parts along dimension 0, may hold values from -6 to 6
- g2m_src: int32 [32, 64], P(('groups', 'dom', 'feat', 'sub')), parts along dimension 0, may hold values from 0 to 511
- g2m_dst: int32 [32, 64], P(('groups', 'dom', 'feat', 'sub')), parts along dimension 0, may hold values from 0 to 511
- g2m_count: int32 [32, 8], P(('groups', 'dom', 'feat', 'sub')), parts along dimension 0, may hold values from 0 to 8, as said below
- g2m_dist: bfloat16 [32, 64], P(('groups', 'dom', 'feat', 'sub')), parts along dimension 0, may hold values from 0.5 to 1.5
- m2m_src: int32 [32, 1536], P(('groups', 'dom', 'feat', 'sub')), parts along dimension 0, may hold values from 0 to 767
- m2m_dst: int32 [32, 1536], P(('groups', 'dom', 'feat', 'sub')), parts along dimension 0, may hold values from 0 to 511
- m2m_count: int32 [32, 1], P(('groups', 'dom', 'feat', 'sub')), parts along dimension 0, may hold values from 512 to 1536, as said below
- m2m_dist: float32 [32, 1536], P(('groups', 'dom', 'feat', 'sub')), parts along dimension 0, may hold values from 0.5 to 1.5
- enc_edge: bfloat16 [2, 512, 512], replicated, may hold values from -0.25 to 0.25
- enc_node_in: bfloat16 [2, 512, 512], replicated, may hold values from -0.25 to 0.25
- enc_node_out: bfloat16 [512, 512], replicated, may hold values from -0.25 to 0.25
- proc_edge: bfloat16 [2, 512, 512], replicated, may hold values from -0.25 to 0.25
- enc_vecs: float32 [3, 512], replicated, may hold values from -3 to 3
- proc_vecs: float32 [2, 512], replicated, may hold values from -3 to 3
Outputs:
- mesh_enc: bfloat16 [8192, 512], P(('groups', 'dom', 'feat', 'sub')), parts along dimension 0
- mesh_agg: bfloat16 [8192, 512], P(('groups', 'dom', 'feat', 'sub')), parts along dimension 0
The draws below stay inside these ranges and needn't reach their ends.
There are 2 independent parts, one for each index of `groups`. The reference program is written for one: setup_inputs(seed, part) draws one part's arguments, and reference() takes and returns one part's arrays. A program takes and returns all parts, laid end to end along the dimension named above; an argument that names none is the same for every part. Nothing has to cross between parts.
Inputs may be any that keep to these rules, and one draw needn't show every extreme that they name: `g2m_count`: in every draw one owner receives 8 live slots from every sender. `m2m_count`: live slots stand at the head of each block; one device's block is full in every draw.
All inputs are finite; a program needn't handle non-finite values.
Results may differ from the reference program's by a relative error of at most 0.0058.
Values may be sent and summed in bfloat16 or wider, within the bound.
A program may use at most 64 MiB of HBM per device.

```python
import jax
import jax.numpy as jnp
from jax import lax

LATENT = 512
HIDDEN_SIZE = 512
GRID_DEV = 512
CAP = 8
M2M_DEV = 1536
RIM = 128
SUBS = 2
OWN = 512
OWNERS = 8
SENDERS = 16
GRID = 8192
MESH = 4096


def draw_g2m_count(key, part):
    key = jax.random.fold_in(key, 11)
    key_light, key_heavy, key_order = jax.random.split(key, 3)
    light_counts = jax.random.randint(key_light, (SENDERS, OWNERS), 0, CAP // 2 + 1)
    heavy_counts = jax.random.randint(key_heavy, (SENDERS, OWNERS), CAP // 2, CAP + 1)
    ordering = jax.random.permutation(key_order, OWNERS)
    marked = jnp.zeros((OWNERS,), jnp.int32).at[ordering[:max(OWNERS // 8, 1)]].set(1)
    counts = jnp.where(marked[None, :] > 0, heavy_counts, light_counts)
    return counts.at[:, ordering[0]].set(CAP).astype(jnp.int32)


def draw_m2m_count(key, part):
    key = jax.random.fold_in(key, 23)
    key_counts, key_full = jax.random.split(key, 2)
    counts = jax.random.randint(key_counts, (SENDERS, 1), M2M_DEV // 3, M2M_DEV + 1)
    full_device = jax.random.randint(key_full, (), 0, SENDERS)
    return counts.at[full_device, 0].set(M2M_DEV).astype(jnp.int32)


def set_ends(values, key, least, high):
    longest = values.shape.index(max(values.shape))
    spots = []
    for shift in (0, 1):
        where = [jax.random.randint(jax.random.fold_in(key, axis), (), 0, length) for axis, length in enumerate(values.shape)]
        where[longest] = (where[longest] + shift) % values.shape[longest]
        spots.append(tuple(where))
    return values.at[spots[0]].set(least).at[spots[1]].set(high)


def level_of(own_key, extent, cuts, least, largest):
    level, own = 1.0, jax.random.fold_in(own_key, 6)
    for dim, parts in cuts:
        steps = jnp.exp(jax.random.uniform(jax.random.fold_in(own, dim), (parts,), jnp.float32, least / len(cuts), largest / len(cuts)))
        level = level * jnp.repeat(steps, extent[dim] // parts).reshape([-1 if axis == dim else 1 for axis in range(len(extent))])
    return level


def centred(own_key, dims, deviation, reach, cuts=(), held_as=jnp.bfloat16):
    result = jax.random.normal(own_key, dims, jnp.float32) * deviation
    if len(cuts) > 0:
        result = level_of(own_key, dims, cuts, -0.22, 0.18) * result
    return jnp.clip(result, min=-reach, max=reach).astype(held_as)


def setup_inputs(seed: int = 0, part: int = 0) -> dict:
    arg_keys = jax.random.split(jax.random.key(seed), 17)
    own_keys = jax.random.split(jax.random.fold_in(arg_keys[16], part), 17)
    return {
        "grid_lat": centred(own_keys[0], (GRID, LATENT), 1.0, 6.0, ((0, 16),)),
        "mesh_lat": centred(own_keys[1], (MESH, LATENT), 1.0, 6.0, ((0, 16),)),
        "g2m_src": set_ends(jax.random.randint(own_keys[2], (SENDERS, OWNERS * CAP), 0, GRID_DEV), jax.random.fold_in(own_keys[2], 1), 0, GRID_DEV - 1).astype(jnp.int32),
        "g2m_dst": set_ends(jax.random.randint(own_keys[3], (SENDERS, OWNERS * CAP), 0, OWN), jax.random.fold_in(own_keys[3], 1), 0, OWN - 1).astype(jnp.int32),
        "g2m_count": draw_g2m_count(jax.random.fold_in(jax.random.fold_in(arg_keys[16], part), 71), part),
        "g2m_dist": jnp.clip(0.5 + 1.0 * jax.random.uniform(own_keys[5], (SENDERS, OWNERS * CAP), jnp.float32) ** level_of(own_keys[5], (SENDERS, OWNERS * CAP), ((0, 16),), -0.2, 0.2), 0.5, 1.5).astype(jnp.bfloat16),
        "m2m_src": set_ends(jax.random.randint(own_keys[6], (SENDERS, M2M_DEV), 0, OWN + 2 * RIM), jax.random.fold_in(own_keys[6], 1), 0, (OWN + 2 * RIM) - 1).astype(jnp.int32),
        "m2m_dst": set_ends(jax.random.randint(own_keys[7], (SENDERS, M2M_DEV), 0, OWN), jax.random.fold_in(own_keys[7], 1), 0, OWN - 1).astype(jnp.int32),
        "m2m_count": draw_m2m_count(jax.random.fold_in(jax.random.fold_in(arg_keys[16], part), 71), part),
        "m2m_dist": jnp.clip(0.5 + 1.0 * jax.random.uniform(own_keys[9], (SENDERS, M2M_DEV), jnp.float32) ** level_of(own_keys[9], (SENDERS, M2M_DEV), ((0, 16),), -0.2, 0.2), 0.5, 1.5),
        "enc_edge": centred(arg_keys[10], (2, LATENT, HIDDEN_SIZE), LATENT ** -0.5, 0.25),
        "enc_node_in": centred(arg_keys[11], (2, LATENT, HIDDEN_SIZE), LATENT ** -0.5, 0.25),
        "enc_node_out": centred(arg_keys[12], (HIDDEN_SIZE, LATENT), HIDDEN_SIZE ** -0.5, 0.25),
        "proc_edge": centred(arg_keys[13], (2, LATENT, HIDDEN_SIZE), LATENT ** -0.5, 0.25),
        "enc_vecs": centred(arg_keys[14], (3, HIDDEN_SIZE), 0.5, 3.0, (), jnp.float32),
        "proc_vecs": centred(arg_keys[15], (2, HIDDEN_SIZE), 0.5, 3.0, (), jnp.float32),
    }


def node_update(own_rows, aggregate, weight_first, weight_second, weight_out, bias_row):
    pre_act = jnp.dot(own_rows, weight_first, preferred_element_type=jnp.float32)
    pre_act = pre_act + jnp.dot(aggregate, weight_second, preferred_element_type=jnp.float32) + bias_row
    hidden_node = jax.nn.silu(pre_act).astype(jnp.bfloat16)
    update = jnp.dot(hidden_node, weight_out, preferred_element_type=jnp.float32)
    return (own_rows.astype(jnp.float32) + update).astype(jnp.bfloat16)


def sum_edges(source_terms, receiver_proj, receivers, lengths, live_mask, sub_ids, section_vectors):
    pre_act = source_terms + receiver_proj[receivers] + lengths.astype(jnp.float32)[..., None] * section_vectors[1] + section_vectors[0]
    rounded_edge = lax.optimization_barrier(jax.nn.silu(pre_act).astype(jnp.bfloat16))
    hidden_edge = jnp.where(live_mask[..., None], rounded_edge.astype(jnp.float32), 0.0)
    partial_value = jnp.zeros((SUBS, OWN, HIDDEN_SIZE), jnp.float32).at[sub_ids, receivers].add(hidden_edge)
    rounded = lax.optimization_barrier(partial_value.astype(jnp.bfloat16))
    return jnp.sum(rounded.astype(jnp.float32), axis=0).astype(jnp.bfloat16)


def reference(grid_lat, mesh_lat, g2m_src, g2m_dst, g2m_count, g2m_dist, m2m_src, m2m_dst, m2m_count, m2m_dist, enc_edge, enc_node_in, enc_node_out, proc_edge, enc_vecs, proc_vecs):
    grid_proj = jnp.dot(grid_lat, enc_edge[0], preferred_element_type=jnp.float32).astype(jnp.bfloat16)
    grid_blocks = grid_proj.reshape(SENDERS, GRID_DEV, HIDDEN_SIZE)
    sender_ids = jnp.arange(SENDERS, dtype=jnp.int32)
    slot_ids = jnp.arange(CAP, dtype=jnp.int32)
    sub_ids = jnp.broadcast_to((sender_ids % SUBS)[:, None], (SENDERS, CAP))

    def by_owner(array):
        return array.reshape(SENDERS, OWNERS, CAP).transpose(1, 0, 2)

    def encode_owner(item):
        own_rows, sources, receivers, lengths, counts = item
        receiver_proj = jnp.dot(own_rows, enc_edge[1], preferred_element_type=jnp.float32)
        source_terms = grid_blocks[sender_ids[:, None], sources].astype(jnp.float32)
        live_mask = slot_ids[None, :] < counts[:, None]
        aggregate = sum_edges(source_terms, receiver_proj, receivers, lengths, live_mask, sub_ids, enc_vecs)
        return node_update(own_rows, aggregate, enc_node_in[0], enc_node_in[1], enc_node_out, enc_vecs[2])

    mesh_enc = lax.map(encode_owner, (mesh_lat.reshape(OWNERS, OWN, LATENT), by_owner(g2m_src), by_owner(g2m_dst), by_owner(g2m_dist), g2m_count.T))
    mesh_enc = mesh_enc.reshape(MESH, LATENT)

    edge_slots = jnp.arange(M2M_DEV, dtype=jnp.int32)
    sub_grid = jnp.broadcast_to(jnp.arange(SUBS, dtype=jnp.int32)[:, None], (SUBS, M2M_DEV))
    owner_ids = jnp.arange(OWNERS, dtype=jnp.int32)
    padded = jnp.pad(mesh_enc, ((RIM, RIM), (0, 0)))

    def process_owner(item):
        owner_index, own_rows, sources, receivers, lengths, counts = item
        extended = lax.dynamic_slice_in_dim(padded, (owner_index * OWN).astype(jnp.int32), OWN + 2 * RIM, 0)
        source_proj = jnp.dot(extended, proc_edge[0], preferred_element_type=jnp.float32)
        receiver_proj = jnp.dot(own_rows, proc_edge[1], preferred_element_type=jnp.float32)
        live_mask = edge_slots[None, :] < counts[:, None]
        return sum_edges(source_proj[sources], receiver_proj, receivers, lengths, live_mask, sub_grid, proc_vecs)

    mesh_agg = lax.map(process_owner, (owner_ids, mesh_enc.reshape(OWNERS, OWN, LATENT), m2m_src.reshape(OWNERS, SUBS, M2M_DEV), m2m_dst.reshape(OWNERS, SUBS, M2M_DEV), m2m_dist.reshape(OWNERS, SUBS, M2M_DEV), m2m_count.reshape(OWNERS, SUBS)))
    return mesh_enc, mesh_agg.reshape(MESH, HIDDEN_SIZE)
```

```python
import functools

import jax
import jax.numpy as jnp
from jax import lax
from jax.experimental import pallas as pl
from jax.experimental.pallas import tpu as pltpu
from jax.sharding import PartitionSpec as P

CAP = 8
RIM = 128
LANES = 128
PARTS = 2
MESH = pl.DeviceIdType.MESH
BF16 = jnp.bfloat16
F32 = jnp.float32


def silu(value):
    half = 0.5 * value
    return half + half * jnp.tanh(half)


def dot(left, right):
    return jnp.dot(left, right, preferred_element_type=F32)


def column(row):
    return jnp.transpose(jnp.broadcast_to(row.astype(F32), (LANES, row.shape[1])))


def lane_ids(rows, block):
    ids = lax.broadcasted_iota(jnp.int32, (rows, LANES), 1) + block * LANES
    return ids.astype(F32)


def one_hot(col, width):
    parts = [
        jnp.where(col == lane_ids(col.shape[0], block), 1.0, 0.0)
        for block in range(width // LANES)
    ]
    return jnp.concatenate(parts, axis=1).astype(BF16)


def kernel(
    owners,
    feats,
    grid_hbm,
    mesh_hbm,
    gsrc_ref,
    gdst_ref,
    gcount_ref,
    gdist_ref,
    msrc_ref,
    mdst_ref,
    mcount_ref,
    mdist_ref,
    we_hbm,
    wn_hbm,
    wo_hbm,
    wp_hbm,
    evec_ref,
    pvec_ref,
    enc_out,
    agg_out,
    grid_ref,
    mesh_ref,
    we_ref,
    wn_ref,
    wo_ref,
    wp_ref,
    msg_ref,
    got_ref,
    got2_ref,
    base_ref,
    hot_ref,
    hot_t_ref,
    ext_ref,
    table_ref,
    acc_ref,
    hid_ref,
    part_ref,
    other_ref,
    load_sem,
    a2a_send,
    a2a_recv,
    fwd_send,
    fwd_recv,
    sib_send,
    sib_recv,
    rim_send,
    rim_recv,
    rfw_send,
    rfw_recv,
    par_send,
    par_recv,
):
    sub = lax.axis_index("sub")
    me = lax.axis_index("dom") * feats + lax.axis_index("feat")
    rows, width = mesh_ref.shape
    half = width // 2
    edges = msrc_ref.shape[1]
    own2 = 2 * rows
    sibling = {"sub": 1 - sub}

    def owner_id(owner):
        return {"dom": lax.div(owner, feats), "feat": lax.rem(owner, feats)}

    def send(src, dst, sems, device):
        return pltpu.make_async_remote_copy(
            src_ref=src,
            dst_ref=dst,
            send_sem=sems[0],
            recv_sem=sems[1],
            device_id=device,
            device_id_type=MESH,
        )

    barrier = pltpu.get_barrier_semaphore()
    pl.semaphore_signal(barrier, inc=1, device_id=sibling, device_id_type=MESH)
    for k in range(1, owners):
        pl.semaphore_signal(
            barrier, inc=1, device_id=owner_id(lax.rem(me + k, owners)), device_id_type=MESH
        )

    pairs = (
        (grid_hbm, grid_ref),
        (we_hbm, we_ref),
        (mesh_hbm, mesh_ref),
        (wn_hbm, wn_ref),
        (wo_hbm, wo_ref),
        (wp_hbm, wp_ref),
    )
    loads = [
        pltpu.make_async_copy(src, dst, load_sem.at[i]) for i, (src, dst) in enumerate(pairs)
    ]
    for load in loads:
        load.start()

    gdst = gdst_ref[...]
    upper = (gdst >= rows).astype(jnp.int32)
    upper_col = column(upper)
    lower_col = column(gdst - rows * upper)
    length_col = column(gdist_ref[...])
    source_hot = one_hot(column(gsrc_ref[...]), grid_ref.shape[0])
    slot = lax.broadcasted_iota(jnp.int32, (CAP, LANES), 0)
    live = jnp.concatenate(
        [jnp.where(slot < gcount_ref[0, o], 1.0, 0.0) for o in range(owners)], axis=0
    )
    lower_col = jnp.where(live > 0.5, lower_col, -1.0)
    loads[0].wait()
    picked = dot(source_hot, grid_ref[...]).astype(BF16)
    loads[1].wait()
    term = dot(picked, we_ref[0])
    term = term + jnp.concatenate([length_col] * (width // LANES), axis=1) * evec_ref[1:2, :]
    term = term + evec_ref[0:1, :]
    top = jnp.concatenate([term[:, :half], lower_col], axis=1)
    bottom = jnp.concatenate([term[:, half:], upper_col], axis=1)
    top = top.reshape(owners, CAP, half + LANES)
    bottom = bottom.reshape(owners, CAP, half + LANES)
    msg_ref[...] = jnp.concatenate([top, bottom], axis=1).astype(BF16)

    pl.semaphore_wait(barrier, owners)
    sends = [
        send(
            msg_ref.at[lax.rem(me + k, owners)],
            got_ref.at[k],
            (a2a_send.at[k], a2a_recv.at[k]),
            owner_id(lax.rem(me + k, owners)),
        )
        for k in range(1, owners)
    ]
    for copy in sends:
        copy.start()
    forwards = [
        send(got_ref.at[k], got2_ref.at[k], (fwd_send.at[k], fwd_recv.at[k]), sibling)
        for k in range(owners)
    ]
    got_ref[0] = msg_ref[me]
    forwards[0].start()

    loads[2].wait()
    receiver_proj = dot(mesh_ref[...], we_ref[1]).astype(BF16)
    loads[3].wait()
    base_ref[...] = dot(mesh_ref[...], wn_ref[0]) + evec_ref[2:3, :]
    edge = lax.broadcasted_iota(jnp.int32, (1, edges), 1)
    tags = jnp.where(edge < mcount_ref[0, 0], mdst_ref[...], -1)
    node = lax.broadcasted_iota(jnp.int32, (own2, edges), 0)
    hot_t_ref[...] = jnp.where(node == tags, 1.0, 0.0).astype(BF16)
    source_col = column(msrc_ref[...])
    hot_ref[:, 0:own2] = one_hot(source_col - RIM, own2)
    hot_ref[:, own2 : 2 * own2] = one_hot(column(tags), own2)
    rim_col = jnp.where(source_col >= own2 + RIM, source_col - own2, source_col)
    inside = (source_col >= RIM) & (source_col < own2 + RIM)
    hot_ref[:, 2 * own2 :] = one_hot(jnp.where(inside, -1.0, rim_col), 2 * RIM)
    length_wide = jnp.concatenate([column(mdist_ref[...])] * (width // LANES), axis=1)
    acc_ref[...] = length_wide * pvec_ref[1:2, :] + pvec_ref[0:1, :]

    for k in range(1, owners):
        sends[k - 1].wait_recv()
        forwards[k].start()
    loads[4].wait()
    loads[5].wait()
    for copy in forwards:
        copy.wait_recv()

    count = owners * CAP
    got = [got_ref[...].astype(F32), got2_ref[...].astype(F32)]
    top = [g[:, 0:CAP, :].reshape(count, half + LANES) for g in got]
    bottom = [g[:, CAP:, :].reshape(count, half + LANES) for g in got]
    top = jnp.concatenate(top, axis=0)
    bottom = jnp.concatenate(bottom, axis=0)
    mine = jnp.where(bottom[:, half:] == sub.astype(F32), top[:, half:], -1.0)
    hot = one_hot(mine, rows)
    pre = jnp.concatenate([top[:, :half], bottom[:, :half]], axis=1) + dot(hot, receiver_proj)
    hidden = silu(pre).astype(BF16)
    aggregate = lax.dot_general(
        hot, hidden, (((0,), (0,)), ((), ())), preferred_element_type=F32
    )
    hid_ref[0:rows, :] = aggregate.astype(BF16)

    own_at = RIM + sub * rows
    piece = RIM // PARTS
    rim_at = (1 - sub) * (RIM + own2)
    step = 2 * sub - 1
    target, source = me + step, me - step
    has_target = (target >= 0) & (target < owners)
    has_source = (source >= 0) & (source < owners)

    def update(start, size):
        at = pl.ds(pl.multiple_of(start, RIM), size)
        value = base_ref[at, :] + dot(hid_ref[at, :], wn_ref[1])
        node_hidden = silu(value).astype(BF16)
        fresh = mesh_ref[at, :].astype(F32) + dot(node_hidden, wo_ref[...])
        fresh = fresh.astype(BF16)
        enc_out[at, :] = fresh
        ext_ref[pl.ds(pl.multiple_of(own_at + start, RIM), size), :] = fresh

    def to_sibling(start, size, index):
        at = pl.ds(pl.multiple_of(own_at + start, RIM), size)
        return send(
            ext_ref.at[at], ext_ref.at[at], (sib_send.at[index], sib_recv.at[index]), sibling
        )

    edge_start, rest_start = sub * (rows - RIM), (1 - sub) * RIM
    update(edge_start, RIM)
    rims = []
    for i in range(PARTS):
        src = pl.ds(pl.multiple_of(own_at + edge_start + i * piece, piece), piece)
        dst = pl.ds(pl.multiple_of(rim_at + i * piece, piece), piece)
        rims.append(
            send(
                ext_ref.at[src],
                ext_ref.at[dst],
                (rim_send.at[i], rim_recv.at[i]),
                owner_id(lax.clamp(0, target, owners - 1)),
            )
        )

    @pl.when(has_target)
    def _():
        for copy in rims:
            copy.start()

    @pl.when(jnp.logical_not(has_source))
    def _():
        ext_ref[pl.ds(pl.multiple_of(rim_at, RIM), RIM), :] = jnp.zeros((RIM, width), BF16)

    shares = [to_sibling(edge_start, RIM, 0), to_sibling(rest_start, rows - RIM, 1)]
    shares[0].start()
    update(rest_start, rows - RIM)
    shares[1].start()

    def project(at, size):
        block = ext_ref[pl.ds(pl.multiple_of(at, RIM), size), :]
        to = pl.multiple_of(at - RIM, RIM)
        table_ref[pl.ds(to, size), :] = dot(block, wp_ref[0]).astype(BF16)
        table_ref[pl.ds(pl.multiple_of(to + own2, RIM), size), :] = dot(
            block, wp_ref[1]
        ).astype(BF16)

    project(own_at, rows)
    shares[0].wait_recv()
    shares[1].wait_recv()
    project(RIM + (1 - sub) * rows, rows)
    chunk = 512
    for at in range(0, edges, chunk):
        acc_ref[at : at + chunk, :] += dot(
            hot_ref[at : at + chunk, 0 : 2 * own2], table_ref[0 : 2 * own2, :]
        )

    passed = []
    for i in range(PARTS):
        at = pl.ds(pl.multiple_of(rim_at + i * piece, piece), piece)
        passed.append(
            send(ext_ref.at[at], ext_ref.at[at], (rfw_send.at[i], rfw_recv.at[i]), sibling)
        )
    for i in range(PARTS):

        @pl.when(has_source)
        def _():
            rims[i].wait_recv()

        passed[i].start()

    def project_rim(at, to):
        block = ext_ref[pl.ds(pl.multiple_of(at, RIM), RIM), :]
        table_ref[pl.ds(pl.multiple_of(2 * own2 + to, RIM), RIM), :] = dot(
            block, wp_ref[0]
        ).astype(BF16)

    project_rim(rim_at, (1 - sub) * RIM)
    for copy in passed:
        copy.wait_recv()
    project_rim(sub * (RIM + own2), sub * RIM)
    for at in range(0, edges, chunk):
        value = acc_ref[at : at + chunk, :] + dot(
            hot_ref[at : at + chunk, 2 * own2 :], table_ref[2 * own2 :, :]
        )
        hid_ref[at : at + chunk, :] = silu(value).astype(BF16)

    def summed(which):
        at = pl.ds(pl.multiple_of(which * rows, RIM), rows)
        return dot(hot_t_ref[at, :], hid_ref[...]).astype(BF16)

    part_ref[...] = summed(1 - sub)
    partial = send(part_ref, other_ref, (par_send.at[0], par_recv.at[0]), sibling)
    partial.start()
    mine = summed(sub).astype(F32)
    partial.wait_recv()
    agg_out[...] = (mine + other_ref[...].astype(F32)).astype(BF16)

    for copy in sends + forwards + shares + passed + [partial]:
        copy.wait_send()

    @pl.when(has_target)
    def _():
        for copy in rims:
            copy.wait_send()


def on_device(owners, feats, *args):
    grid_lat, mesh_lat = args[0], args[1]
    edges, slots = args[6].shape[1], args[2].shape[1]
    rows, width = mesh_lat.shape
    own2 = 2 * rows
    vmem = pl.BlockSpec(memory_space=pltpu.VMEM)
    smem = pl.BlockSpec(memory_space=pltpu.SMEM)
    hbm = pl.BlockSpec(memory_space=pl.ANY)
    in_specs = [hbm, hbm, vmem, vmem, smem, vmem, vmem, vmem, smem, vmem]
    in_specs += [hbm] * 4 + [vmem] * 2
    message = (owners, 2 * CAP, width // 2 + LANES)
    dma = pltpu.SemaphoreType.DMA
    scratch = [
        pltpu.VMEM(grid_lat.shape, BF16),
        pltpu.VMEM(mesh_lat.shape, BF16),
        pltpu.VMEM(args[10].shape, BF16),
        pltpu.VMEM(args[11].shape, BF16),
        pltpu.VMEM(args[12].shape, BF16),
        pltpu.VMEM(args[13].shape, BF16),
        pltpu.VMEM(message, BF16),
        pltpu.VMEM(message, BF16),
        pltpu.VMEM(message, BF16),
        pltpu.VMEM((rows, width), F32),
        pltpu.VMEM((edges, 2 * own2 + 2 * RIM), BF16),
        pltpu.VMEM((own2, edges), BF16),
        pltpu.VMEM((own2 + 2 * RIM, width), BF16),
        pltpu.VMEM((2 * own2 + 2 * RIM, width), BF16),
        pltpu.VMEM((edges, width), F32),
        pltpu.VMEM((edges, width), BF16),
        pltpu.VMEM((rows, width), BF16),
        pltpu.VMEM((rows, width), BF16),
        dma((6,)),
        dma((owners,)),
        dma((owners,)),
        dma((owners,)),
        dma((owners,)),
        dma((2,)),
        dma((2,)),
        dma((PARTS,)),
        dma((PARTS,)),
        dma((PARTS,)),
        dma((PARTS,)),
        dma((1,)),
        dma((1,)),
    ]
    return pl.pallas_call(
        functools.partial(kernel, owners, feats),
        out_shape=[jax.ShapeDtypeStruct((rows, width), BF16)] * 2,
        in_specs=in_specs,
        out_specs=[vmem, vmem],
        scratch_shapes=scratch,
        compiler_params=pltpu.CompilerParams(
            collective_id=0, has_side_effects=True, vmem_limit_bytes=40 * 1024 * 1024
        ),
    )(*args)


def solution(mesh):
    split = P(("groups", "dom", "feat", "sub"), None)
    feats = mesh.shape["feat"]
    owners = mesh.shape["dom"] * feats
    return jax.shard_map(
        functools.partial(on_device, owners, feats),
        mesh=mesh,
        in_specs=(split,) * 10 + (P(),) * 6,
        out_specs=(split, split),
        check_vma=False,
    )
```

```python
import functools

import jax
import jax.numpy as jnp
from jax import lax
from jax.experimental import pallas as pl
from jax.experimental.pallas import tpu as pltpu
from jax.sharding import PartitionSpec as P

CAP = 8
RIM = 128
LANES = 128
PARTS = 2
LIMIT = 63 * 1024 * 1024
MESH = pl.DeviceIdType.MESH
BF16 = jnp.bfloat16
F32 = jnp.float32


def silu(value):
    half = 0.5 * value
    return half + half * jnp.tanh(half)


def dot(left, right):
    return jnp.dot(left, right, preferred_element_type=F32)


def column(row):
    return jnp.transpose(jnp.broadcast_to(row.astype(F32), (LANES, row.shape[1])))


def lane_ids(rows, block):
    ids = lax.broadcasted_iota(jnp.int32, (rows, LANES), 1) + block * LANES
    return ids.astype(F32)


def one_hot(col, width):
    parts = [
        jnp.where(col == lane_ids(col.shape[0], block), 1.0, 0.0)
        for block in range(width // LANES)
    ]
    return jnp.concatenate(parts, axis=1).astype(BF16)


def kernel(
    owners,
    feats,
    grid_hbm,
    mesh_hbm,
    gsrc_hbm,
    gdst_hbm,
    gcount_hbm,
    gdist_hbm,
    msrc_hbm,
    mdst_hbm,
    mcount_hbm,
    mdist_hbm,
    we_hbm,
    wn_hbm,
    wo_hbm,
    wp_hbm,
    evec_hbm,
    pvec_hbm,
    enc_out,
    agg_out,
    gsrc_ref,
    gdst_ref,
    gcount_ref,
    gdist_ref,
    msrc_ref,
    mdst_ref,
    mcount_ref,
    mdist_ref,
    evec_ref,
    pvec_ref,
    grid_ref,
    mesh_ref,
    we_ref,
    wn_ref,
    wo_ref,
    wp_ref,
    msg_ref,
    got_ref,
    got2_ref,
    base_ref,
    hot_ref,
    hot_t_ref,
    ext_ref,
    table_ref,
    acc_ref,
    hid_ref,
    part_ref,
    other_ref,
    enc_ref,
    agg_ref,
    load_sem,
    a2a_send,
    a2a_recv,
    fwd_send,
    fwd_recv,
    sib_send,
    sib_recv,
    rim_send,
    rim_recv,
    rfw_send,
    rfw_recv,
    par_send,
    par_recv,
):
    sub = lax.axis_index("sub")
    me = lax.axis_index("dom") * feats + lax.axis_index("feat")
    rows, width = mesh_ref.shape
    half = width // 2
    edges = msrc_ref.shape[1]
    own2 = 2 * rows
    sibling = {"sub": 1 - sub}

    def owner_id(owner):
        return {"dom": lax.div(owner, feats), "feat": lax.rem(owner, feats)}

    def send(src, dst, sems, device):
        return pltpu.make_async_remote_copy(
            src_ref=src,
            dst_ref=dst,
            send_sem=sems[0],
            recv_sem=sems[1],
            device_id=device,
            device_id_type=MESH,
        )

    barrier = pltpu.get_barrier_semaphore()
    pl.semaphore_signal(barrier, inc=1, device_id=sibling, device_id_type=MESH)
    for k in range(1, owners):
        pl.semaphore_signal(
            barrier, inc=1, device_id=owner_id(lax.rem(me + k, owners)), device_id_type=MESH
        )

    pairs = (
        (gsrc_hbm, gsrc_ref),
        (grid_hbm, grid_ref),
        (we_hbm.at[0], we_ref.at[0]),
        (gdst_hbm, gdst_ref),
        (gcount_hbm, gcount_ref),
        (gdist_hbm, gdist_ref),
        (evec_hbm, evec_ref),
        (mesh_hbm, mesh_ref),
        (we_hbm.at[1], we_ref.at[1]),
        (wn_hbm, wn_ref),
        (msrc_hbm, msrc_ref),
        (mdst_hbm, mdst_ref),
        (mcount_hbm, mcount_ref),
        (mdist_hbm, mdist_ref),
        (pvec_hbm, pvec_ref),
        (wo_hbm, wo_ref),
        (wp_hbm, wp_ref),
    )
    loads = [
        pltpu.make_async_copy(src, dst, load_sem.at[i]) for i, (src, dst) in enumerate(pairs)
    ]
    for load in loads[:7]:
        load.start()

    def loaded(first, last):
        for load in loads[first : last + 1]:
            load.wait()

    loaded(0, 0)
    source_hot = one_hot(column(gsrc_ref[...]), grid_ref.shape[0])
    loaded(1, 1)
    picked = dot(source_hot, grid_ref[...]).astype(BF16)
    loaded(2, 2)
    for load in loads[7:]:
        load.start()
    term = dot(picked, we_ref[0])
    loaded(3, 6)

    gdst = gdst_ref[...]
    upper = (gdst >= rows).astype(jnp.int32)
    upper_col = column(upper)
    lower_col = column(gdst - rows * upper)
    length_col = column(gdist_ref[...])
    slot = lax.broadcasted_iota(jnp.int32, (CAP, LANES), 0)
    live = jnp.concatenate(
        [jnp.where(slot < gcount_ref[0, o], 1.0, 0.0) for o in range(owners)], axis=0
    )
    lower_col = jnp.where(live > 0.5, lower_col, -1.0)
    term = term + jnp.concatenate([length_col] * (width // LANES), axis=1) * evec_ref[1:2, :]
    term = term + evec_ref[0:1, :]
    top = jnp.concatenate([term[:, :half], lower_col], axis=1)
    bottom = jnp.concatenate([term[:, half:], upper_col], axis=1)
    top = top.reshape(owners, CAP, half + LANES)
    bottom = bottom.reshape(owners, CAP, half + LANES)
    msg_ref[...] = jnp.concatenate([top, bottom], axis=1).astype(BF16)

    pl.semaphore_wait(barrier, owners)
    sends = [
        send(
            msg_ref.at[lax.rem(me + k, owners)],
            got_ref.at[k],
            (a2a_send.at[k], a2a_recv.at[k]),
            owner_id(lax.rem(me + k, owners)),
        )
        for k in range(1, owners)
    ]
    for copy in sends:
        copy.start()
    forwards = [
        send(got_ref.at[k], got2_ref.at[k], (fwd_send.at[k], fwd_recv.at[k]), sibling)
        for k in range(owners)
    ]
    got_ref[0] = msg_ref[me]
    forwards[0].start()

    loaded(7, 8)
    receiver_proj = dot(mesh_ref[...], we_ref[1]).astype(BF16)
    loaded(9, 9)
    base_ref[...] = dot(mesh_ref[...], wn_ref[0]) + evec_ref[2:3, :]
    loaded(10, 14)
    edge = lax.broadcasted_iota(jnp.int32, (1, edges), 1)
    tags = jnp.where(edge < mcount_ref[0, 0], mdst_ref[...], -1)
    node = lax.broadcasted_iota(jnp.int32, (own2, edges), 0)
    hot_t_ref[...] = jnp.where(node == tags, 1.0, 0.0).astype(BF16)
    source_col = column(msrc_ref[...])
    hot_ref[:, 0:own2] = one_hot(source_col - RIM, own2)
    hot_ref[:, own2 : 2 * own2] = one_hot(column(tags), own2)
    rim_col = jnp.where(source_col >= own2 + RIM, source_col - own2, source_col)
    inside = (source_col >= RIM) & (source_col < own2 + RIM)
    hot_ref[:, 2 * own2 :] = one_hot(jnp.where(inside, -1.0, rim_col), 2 * RIM)
    length_wide = jnp.concatenate([column(mdist_ref[...])] * (width // LANES), axis=1)
    acc_ref[...] = length_wide * pvec_ref[1:2, :] + pvec_ref[0:1, :]

    for k in range(1, owners):
        sends[k - 1].wait_recv()
        forwards[k].start()
    loaded(15, 16)
    for copy in forwards:
        copy.wait_recv()

    count = owners * CAP
    got = [got_ref[...].astype(F32), got2_ref[...].astype(F32)]
    top = [g[:, 0:CAP, :].reshape(count, half + LANES) for g in got]
    bottom = [g[:, CAP:, :].reshape(count, half + LANES) for g in got]
    top = jnp.concatenate(top, axis=0)
    bottom = jnp.concatenate(bottom, axis=0)
    mine = jnp.where(bottom[:, half:] == sub.astype(F32), top[:, half:], -1.0)
    hot = one_hot(mine, rows)
    pre = jnp.concatenate([top[:, :half], bottom[:, :half]], axis=1) + dot(hot, receiver_proj)
    hidden = silu(pre).astype(BF16)
    aggregate = lax.dot_general(
        hot, hidden, (((0,), (0,)), ((), ())), preferred_element_type=F32
    )
    hid_ref[0:rows, :] = aggregate.astype(BF16)

    own_at = RIM + sub * rows
    piece = RIM // PARTS
    rim_at = (1 - sub) * (RIM + own2)
    step = 2 * sub - 1
    target, source = me + step, me - step
    has_target = (target >= 0) & (target < owners)
    has_source = (source >= 0) & (source < owners)

    def update(start, size):
        at = pl.ds(pl.multiple_of(start, RIM), size)
        value = base_ref[at, :] + dot(hid_ref[at, :], wn_ref[1])
        node_hidden = silu(value).astype(BF16)
        fresh = mesh_ref[at, :].astype(F32) + dot(node_hidden, wo_ref[...])
        fresh = fresh.astype(BF16)
        enc_ref[at, :] = fresh
        ext_ref[pl.ds(pl.multiple_of(own_at + start, RIM), size), :] = fresh

    def to_sibling(start, size, index):
        at = pl.ds(pl.multiple_of(own_at + start, RIM), size)
        return send(
            ext_ref.at[at], ext_ref.at[at], (sib_send.at[index], sib_recv.at[index]), sibling
        )

    edge_start, rest_start = sub * (rows - RIM), (1 - sub) * RIM
    update(edge_start, RIM)
    rims = []
    for i in range(PARTS):
        src = pl.ds(pl.multiple_of(own_at + edge_start + i * piece, piece), piece)
        dst = pl.ds(pl.multiple_of(rim_at + i * piece, piece), piece)
        rims.append(
            send(
                ext_ref.at[src],
                ext_ref.at[dst],
                (rim_send.at[i], rim_recv.at[i]),
                owner_id(lax.clamp(0, target, owners - 1)),
            )
        )

    @pl.when(has_target)
    def _():
        for copy in rims:
            copy.start()

    @pl.when(jnp.logical_not(has_source))
    def _():
        ext_ref[pl.ds(pl.multiple_of(rim_at, RIM), RIM), :] = jnp.zeros((RIM, width), BF16)

    shares = [to_sibling(edge_start, RIM, 0), to_sibling(rest_start, rows - RIM, 1)]
    shares[0].start()
    update(rest_start, rows - RIM)
    shares[1].start()
    enc_store = pltpu.make_async_copy(enc_ref, enc_out, load_sem.at[0])
    enc_store.start()

    def project(at, size):
        block = ext_ref[pl.ds(pl.multiple_of(at, RIM), size), :]
        to = pl.multiple_of(at - RIM, RIM)
        table_ref[pl.ds(to, size), :] = dot(block, wp_ref[0]).astype(BF16)
        table_ref[pl.ds(pl.multiple_of(to + own2, RIM), size), :] = dot(
            block, wp_ref[1]
        ).astype(BF16)

    project(own_at, rows)
    shares[0].wait_recv()
    shares[1].wait_recv()
    project(RIM + (1 - sub) * rows, rows)
    chunk = 512
    for at in range(0, edges, chunk):
        acc_ref[at : at + chunk, :] += dot(
            hot_ref[at : at + chunk, 0 : 2 * own2], table_ref[0 : 2 * own2, :]
        )

    passed = []
    for i in range(PARTS):
        at = pl.ds(pl.multiple_of(rim_at + i * piece, piece), piece)
        passed.append(
            send(ext_ref.at[at], ext_ref.at[at], (rfw_send.at[i], rfw_recv.at[i]), sibling)
        )
    for i in range(PARTS):

        @pl.when(has_source)
        def _():
            rims[i].wait_recv()

        passed[i].start()

    def project_rim(at, to):
        block = ext_ref[pl.ds(pl.multiple_of(at, RIM), RIM), :]
        table_ref[pl.ds(pl.multiple_of(2 * own2 + to, RIM), RIM), :] = dot(
            block, wp_ref[0]
        ).astype(BF16)

    project_rim(rim_at, (1 - sub) * RIM)
    for copy in passed:
        copy.wait_recv()
    project_rim(sub * (RIM + own2), sub * RIM)
    for at in range(0, edges, chunk):
        value = acc_ref[at : at + chunk, :] + dot(
            hot_ref[at : at + chunk, 2 * own2 :], table_ref[2 * own2 :, :]
        )
        hid_ref[at : at + chunk, :] = silu(value).astype(BF16)

    def summed(which):
        at = pl.ds(pl.multiple_of(which * rows, RIM), rows)
        return dot(hot_t_ref[at, :], hid_ref[...]).astype(BF16)

    part_ref[...] = summed(1 - sub)
    partial = send(part_ref, other_ref, (par_send.at[0], par_recv.at[0]), sibling)
    partial.start()
    mine = summed(sub).astype(F32)
    partial.wait_recv()
    agg_ref[...] = (mine + other_ref[...].astype(F32)).astype(BF16)
    agg_store = pltpu.make_async_copy(agg_ref, agg_out, load_sem.at[1])
    agg_store.start()

    for copy in sends + forwards + shares + passed + [partial]:
        copy.wait_send()

    @pl.when(has_target)
    def _():
        for copy in rims:
            copy.wait_send()

    enc_store.wait()
    agg_store.wait()


def finish(enc_in, agg_in, enc_out, agg_out, enc_ref, agg_ref, sems):
    reads = [
        pltpu.make_async_copy(enc_in, enc_ref, sems.at[0]),
        pltpu.make_async_copy(agg_in, agg_ref, sems.at[1]),
    ]
    writes = [
        pltpu.make_async_copy(enc_ref, enc_out, sems.at[2]),
        pltpu.make_async_copy(agg_ref, agg_out, sems.at[3]),
    ]
    for copy in reads:
        copy.start()
    for read, write in zip(reads, writes):
        read.wait()
        write.start()
    for copy in writes:
        copy.wait()


def on_device(owners, feats, *args):
    grid_lat, mesh_lat = args[0], args[1]
    edges, slots = args[6].shape[1], args[2].shape[1]
    rows, width = mesh_lat.shape
    own2 = 2 * rows
    hbm = pl.BlockSpec(memory_space=pltpu.HBM)
    message = (owners, 2 * CAP, width // 2 + LANES)
    dma = pltpu.SemaphoreType.DMA
    small = [args[i] for i in (2, 3, 4, 5, 6, 7, 8, 9, 14, 15)]
    scratch = [
        (pltpu.SMEM if i in (2, 6) else pltpu.VMEM)(a.shape, a.dtype)
        for i, a in enumerate(small)
    ]
    scratch += [
        pltpu.VMEM(grid_lat.shape, BF16),
        pltpu.VMEM(mesh_lat.shape, BF16),
        pltpu.VMEM(args[10].shape, BF16),
        pltpu.VMEM(args[11].shape, BF16),
        pltpu.VMEM(args[12].shape, BF16),
        pltpu.VMEM(args[13].shape, BF16),
        pltpu.VMEM(message, BF16),
        pltpu.VMEM(message, BF16),
        pltpu.VMEM(message, BF16),
        pltpu.VMEM((rows, width), F32),
        pltpu.VMEM((edges, 2 * own2 + 2 * RIM), BF16),
        pltpu.VMEM((own2, edges), BF16),
        pltpu.VMEM((own2 + 2 * RIM, width), BF16),
        pltpu.VMEM((2 * own2 + 2 * RIM, width), BF16),
        pltpu.VMEM((edges, width), F32),
        pltpu.VMEM((edges, width), BF16),
        pltpu.VMEM((rows, width), BF16),
        pltpu.VMEM((rows, width), BF16),
        pltpu.VMEM((rows, width), BF16),
        pltpu.VMEM((rows, width), BF16),
        dma((17,)),
        dma((owners,)),
        dma((owners,)),
        dma((owners,)),
        dma((owners,)),
        dma((2,)),
        dma((2,)),
        dma((PARTS,)),
        dma((PARTS,)),
        dma((PARTS,)),
        dma((PARTS,)),
        dma((1,)),
        dma((1,)),
    ]
    shapes = [jax.ShapeDtypeStruct((rows, width), BF16)] * 2
    outs = pl.pallas_call(
        functools.partial(kernel, owners, feats),
        out_shape=shapes,
        in_specs=[hbm] * 16,
        out_specs=[hbm, hbm],
        scratch_shapes=scratch,
        compiler_params=pltpu.CompilerParams(
            collective_id=0, has_side_effects=True, vmem_limit_bytes=LIMIT
        ),
    )(*args)
    return pl.pallas_call(
        finish,
        out_shape=shapes,
        in_specs=[hbm, hbm],
        out_specs=[hbm, hbm],
        scratch_shapes=[pltpu.VMEM((rows, width), BF16)] * 2 + [dma((4,))],
    )(*outs)


def solution(mesh):
    split = P(("groups", "dom", "feat", "sub"), None)
    feats = mesh.shape["feat"]
    owners = mesh.shape["dom"] * feats
    return jax.shard_map(
        functools.partial(on_device, owners, feats),
        mesh=mesh,
        in_specs=(split,) * 10 + (P(),) * 6,
        out_specs=(split, split),
        check_vma=False,
    )
```

```python
import functools

import jax
import jax.numpy as jnp
from jax import lax
from jax.experimental import pallas as pl
from jax.experimental.pallas import tpu as pltpu
from jax.sharding import PartitionSpec as P

CAP = 8
RIM = 128
LANES = 128
PARTS = 2
LIMIT = 63 * 1024 * 1024
MESH = pl.DeviceIdType.MESH
BF16 = jnp.bfloat16
F32 = jnp.float32


def silu(value):
    half = 0.5 * value
    return half + half * jnp.tanh(half)


def dot(left, right):
    return jnp.dot(left, right, preferred_element_type=F32)


def column(row):
    return jnp.transpose(jnp.broadcast_to(row.astype(F32), (LANES, row.shape[1])))


def lane_ids(rows, block):
    ids = lax.broadcasted_iota(jnp.int32, (rows, LANES), 1) + block * LANES
    return ids.astype(F32)


def one_hot(col, width):
    parts = [
        jnp.where(col == lane_ids(col.shape[0], block), 1.0, 0.0)
        for block in range(width // LANES)
    ]
    return jnp.concatenate(parts, axis=1).astype(BF16)


def kernel(
    owners,
    feats,
    grid_hbm,
    mesh_hbm,
    gsrc_hbm,
    gdst_hbm,
    gcount_hbm,
    gdist_hbm,
    msrc_hbm,
    mdst_hbm,
    mcount_hbm,
    mdist_hbm,
    we_hbm,
    wn_hbm,
    wo_hbm,
    wp_hbm,
    evec_hbm,
    pvec_hbm,
    enc_out,
    agg_out,
    gsrc_ref,
    gdst_ref,
    gcount_ref,
    gdist_ref,
    msrc_ref,
    mdst_ref,
    mcount_ref,
    mdist_ref,
    evec_ref,
    pvec_ref,
    grid_ref,
    mesh_ref,
    we_ref,
    wn_ref,
    wo_ref,
    wp_ref,
    msg_ref,
    got_ref,
    got2_ref,
    base_ref,
    hot_ref,
    hot_t_ref,
    ext_ref,
    table_ref,
    acc_ref,
    hid_ref,
    part_ref,
    other_ref,
    enc_ref,
    agg_ref,
    load_sem,
    a2a_send,
    a2a_recv,
    fwd_send,
    fwd_recv,
    sib_send,
    sib_recv,
    rim_send,
    rim_recv,
    rfw_send,
    rfw_recv,
    par_send,
    par_recv,
):
    sub = lax.axis_index("sub")
    me = lax.axis_index("dom") * feats + lax.axis_index("feat")
    rows, width = mesh_ref.shape
    half = width // 2
    edges = msrc_ref.shape[1]
    own2 = 2 * rows
    sibling = {"sub": 1 - sub}

    def owner_id(owner):
        return {"dom": lax.div(owner, feats), "feat": lax.rem(owner, feats)}

    def send(src, dst, sems, device):
        return pltpu.make_async_remote_copy(
            src_ref=src,
            dst_ref=dst,
            send_sem=sems[0],
            recv_sem=sems[1],
            device_id=device,
            device_id_type=MESH,
        )

    barrier = pltpu.get_barrier_semaphore()
    pl.semaphore_signal(barrier, inc=1, device_id=sibling, device_id_type=MESH)
    for k in range(1, owners):
        pl.semaphore_signal(
            barrier, inc=1, device_id=owner_id(lax.rem(me + k, owners)), device_id_type=MESH
        )

    pairs = (
        (gsrc_hbm, gsrc_ref),
        (grid_hbm, grid_ref),
        (we_hbm.at[0], we_ref.at[0]),
        (gdst_hbm, gdst_ref),
        (gcount_hbm, gcount_ref),
        (gdist_hbm, gdist_ref),
        (evec_hbm, evec_ref),
        (mesh_hbm, mesh_ref),
        (we_hbm.at[1], we_ref.at[1]),
        (wn_hbm, wn_ref),
        (msrc_hbm, msrc_ref),
        (mdst_hbm, mdst_ref),
        (mcount_hbm, mcount_ref),
        (mdist_hbm, mdist_ref),
        (pvec_hbm, pvec_ref),
        (wo_hbm, wo_ref),
        (wp_hbm, wp_ref),
    )
    loads = [
        pltpu.make_async_copy(src, dst, load_sem.at[i]) for i, (src, dst) in enumerate(pairs)
    ]
    for load in loads[:7]:
        load.start()

    def loaded(first, last):
        for load in loads[first : last + 1]:
            load.wait()

    loaded(0, 0)
    source_hot = one_hot(column(gsrc_ref[...]), grid_ref.shape[0])
    loaded(1, 1)
    picked = dot(source_hot, grid_ref[...]).astype(BF16)
    loaded(2, 2)
    for load in loads[7:]:
        load.start()
    term = dot(picked, we_ref[0])
    loaded(3, 6)

    gdst = gdst_ref[...]
    upper = (gdst >= rows).astype(jnp.int32)
    upper_col = column(upper)
    lower_col = column(gdst - rows * upper)
    length_col = column(gdist_ref[...])
    slot = lax.broadcasted_iota(jnp.int32, (CAP, LANES), 0)
    live = jnp.concatenate(
        [jnp.where(slot < gcount_ref[0, o], 1.0, 0.0) for o in range(owners)], axis=0
    )
    lower_col = jnp.where(live > 0.5, lower_col, -1.0)
    term = term + jnp.concatenate([length_col] * (width // LANES), axis=1) * evec_ref[1:2, :]
    term = term + evec_ref[0:1, :]
    top = jnp.concatenate([term[:, :half], lower_col], axis=1)
    bottom = jnp.concatenate([term[:, half:], upper_col], axis=1)
    top = top.reshape(owners, CAP, half + LANES)
    bottom = bottom.reshape(owners, CAP, half + LANES)
    msg_ref[...] = jnp.concatenate([top, bottom], axis=1).astype(BF16)

    pl.semaphore_wait(barrier, owners)
    sends = [
        send(
            msg_ref.at[lax.rem(me + k, owners)],
            got_ref.at[k],
            (a2a_send.at[k], a2a_recv.at[k]),
            owner_id(lax.rem(me + k, owners)),
        )
        for k in range(1, owners)
    ]
    for copy in sends:
        copy.start()
    forwards = [
        send(got_ref.at[k], got2_ref.at[k], (fwd_send.at[k], fwd_recv.at[k]), sibling)
        for k in range(owners)
    ]
    got_ref[0] = msg_ref[me]
    forwards[0].start()

    loaded(7, 8)
    receiver_proj = dot(mesh_ref[...], we_ref[1]).astype(BF16)
    loaded(9, 9)
    base_ref[...] = dot(mesh_ref[...], wn_ref[0]) + evec_ref[2:3, :]
    loaded(10, 14)
    edge = lax.broadcasted_iota(jnp.int32, (1, edges), 1)
    tags = jnp.where(edge < mcount_ref[0, 0], mdst_ref[...], -1)
    node = lax.broadcasted_iota(jnp.int32, (own2, edges), 0)
    hot_t_ref[...] = jnp.where(node == tags, 1.0, 0.0).astype(BF16)
    source_col = column(msrc_ref[...])
    hot_ref[:, 0:own2] = one_hot(source_col - RIM, own2)
    hot_ref[:, own2 : 2 * own2] = one_hot(column(tags), own2)
    rim_col = jnp.where(source_col >= own2 + RIM, source_col - own2, source_col)
    inside = (source_col >= RIM) & (source_col < own2 + RIM)
    hot_ref[:, 2 * own2 :] = one_hot(jnp.where(inside, -1.0, rim_col), 2 * RIM)
    length_wide = jnp.concatenate([column(mdist_ref[...])] * (width // LANES), axis=1)
    acc_ref[...] = length_wide * pvec_ref[1:2, :] + pvec_ref[0:1, :]

    for k in range(1, owners):
        sends[k - 1].wait_recv()
        forwards[k].start()
    loaded(15, 16)
    for copy in forwards:
        copy.wait_recv()

    count = owners * CAP
    got = [got_ref[...].astype(F32), got2_ref[...].astype(F32)]
    top = [g[:, 0:CAP, :].reshape(count, half + LANES) for g in got]
    bottom = [g[:, CAP:, :].reshape(count, half + LANES) for g in got]
    top = jnp.concatenate(top, axis=0)
    bottom = jnp.concatenate(bottom, axis=0)
    mine = jnp.where(bottom[:, half:] == sub.astype(F32), top[:, half:], -1.0)
    hot = one_hot(mine, rows)
    pre = jnp.concatenate([top[:, :half], bottom[:, :half]], axis=1) + dot(hot, receiver_proj)
    hidden = silu(pre).astype(BF16)
    aggregate = lax.dot_general(
        hot, hidden, (((0,), (0,)), ((), ())), preferred_element_type=F32
    )
    hid_ref[0:rows, :] = aggregate.astype(BF16)

    own_at = RIM + sub * rows
    piece = RIM // PARTS
    rim_at = (1 - sub) * (RIM + own2)
    step = 2 * sub - 1
    target, source = me + step, me - step
    has_target = (target >= 0) & (target < owners)
    has_source = (source >= 0) & (source < owners)

    def update(start, size):
        at = pl.ds(pl.multiple_of(start, RIM), size)
        value = base_ref[at, :] + dot(hid_ref[at, :], wn_ref[1])
        node_hidden = silu(value).astype(BF16)
        fresh = mesh_ref[at, :].astype(F32) + dot(node_hidden, wo_ref[...])
        fresh = fresh.astype(BF16)
        enc_ref[at, :] = fresh
        ext_ref[pl.ds(pl.multiple_of(own_at + start, RIM), size), :] = fresh

    def to_sibling(start, size, index):
        at = pl.ds(pl.multiple_of(own_at + start, RIM), size)
        return send(
            ext_ref.at[at], ext_ref.at[at], (sib_send.at[index], sib_recv.at[index]), sibling
        )

    edge_start, rest_start = sub * (rows - RIM), (1 - sub) * RIM
    update(edge_start, RIM)
    rims = []
    for i in range(PARTS):
        src = pl.ds(pl.multiple_of(own_at + edge_start + i * piece, piece), piece)
        dst = pl.ds(pl.multiple_of(rim_at + i * piece, piece), piece)
        rims.append(
            send(
                ext_ref.at[src],
                ext_ref.at[dst],
                (rim_send.at[i], rim_recv.at[i]),
                owner_id(lax.clamp(0, target, owners - 1)),
            )
        )

    @pl.when(has_target)
    def _():
        for copy in rims:
            copy.start()

    @pl.when(jnp.logical_not(has_source))
    def _():
        ext_ref[pl.ds(pl.multiple_of(rim_at, RIM), RIM), :] = jnp.zeros((RIM, width), BF16)

    shares = [to_sibling(edge_start, RIM, 0), to_sibling(rest_start, rows - RIM, 1)]
    shares[0].start()
    update(rest_start, rows - RIM)
    shares[1].start()
    enc_store = pltpu.make_async_copy(enc_ref, enc_out, load_sem.at[0])
    enc_store.start()

    def project(at, size):
        block = ext_ref[pl.ds(pl.multiple_of(at, RIM), size), :]
        to = pl.multiple_of(at - RIM, RIM)
        table_ref[pl.ds(to, size), :] = dot(block, wp_ref[0]).astype(BF16)
        table_ref[pl.ds(pl.multiple_of(to + own2, RIM), size), :] = dot(
            block, wp_ref[1]
        ).astype(BF16)

    project(own_at, rows)
    shares[0].wait_recv()
    shares[1].wait_recv()
    project(RIM + (1 - sub) * rows, rows)
    passed = []
    for i in range(PARTS):
        at = pl.ds(pl.multiple_of(rim_at + i * piece, piece), piece)
        passed.append(
            send(ext_ref.at[at], ext_ref.at[at], (rfw_send.at[i], rfw_recv.at[i]), sibling)
        )
    chunk = 512
    for at in range(0, edges, chunk):
        acc_ref[at : at + chunk, :] += dot(
            hot_ref[at : at + chunk, 0 : 2 * own2], table_ref[0 : 2 * own2, :]
        )
        if at == 0:
            for i in range(PARTS):

                @pl.when(has_source)
                def _():
                    rims[i].wait_recv()

                passed[i].start()

    def project_rim(at, to):
        block = ext_ref[pl.ds(pl.multiple_of(at, RIM), RIM), :]
        table_ref[pl.ds(pl.multiple_of(2 * own2 + to, RIM), RIM), :] = dot(
            block, wp_ref[0]
        ).astype(BF16)

    project_rim(rim_at, (1 - sub) * RIM)
    for copy in passed:
        copy.wait_recv()
    project_rim(sub * (RIM + own2), sub * RIM)
    for at in range(0, edges, chunk):
        value = acc_ref[at : at + chunk, :] + dot(
            hot_ref[at : at + chunk, 2 * own2 :], table_ref[2 * own2 :, :]
        )
        hid_ref[at : at + chunk, :] = silu(value).astype(BF16)

    def summed(which):
        at = pl.ds(pl.multiple_of(which * rows, RIM), rows)
        return dot(hot_t_ref[at, :], hid_ref[...]).astype(BF16)

    part_ref[...] = summed(1 - sub)
    partial = send(part_ref, other_ref, (par_send.at[0], par_recv.at[0]), sibling)
    partial.start()
    mine = summed(sub).astype(F32)
    partial.wait_recv()
    agg_ref[...] = (mine + other_ref[...].astype(F32)).astype(BF16)
    agg_store = pltpu.make_async_copy(agg_ref, agg_out, load_sem.at[1])
    agg_store.start()

    for copy in sends + forwards + shares + passed + [partial]:
        copy.wait_send()

    @pl.when(has_target)
    def _():
        for copy in rims:
            copy.wait_send()

    enc_store.wait()
    agg_store.wait()


def finish(enc_in, agg_in, enc_out, agg_out, enc_ref, agg_ref, sems):
    reads = [
        pltpu.make_async_copy(enc_in, enc_ref, sems.at[0]),
        pltpu.make_async_copy(agg_in, agg_ref, sems.at[1]),
    ]
    writes = [
        pltpu.make_async_copy(enc_ref, enc_out, sems.at[2]),
        pltpu.make_async_copy(agg_ref, agg_out, sems.at[3]),
    ]
    for copy in reads:
        copy.start()
    for read, write in zip(reads, writes):
        read.wait()
        write.start()
    for copy in writes:
        copy.wait()


def on_device(owners, feats, *args):
    grid_lat, mesh_lat = args[0], args[1]
    edges, slots = args[6].shape[1], args[2].shape[1]
    rows, width = mesh_lat.shape
    own2 = 2 * rows
    hbm = pl.BlockSpec(memory_space=pltpu.HBM)
    message = (owners, 2 * CAP, width // 2 + LANES)
    dma = pltpu.SemaphoreType.DMA
    small = [args[i] for i in (2, 3, 4, 5, 6, 7, 8, 9, 14, 15)]
    scratch = [
        (pltpu.SMEM if i in (2, 6) else pltpu.VMEM)(a.shape, a.dtype)
        for i, a in enumerate(small)
    ]
    scratch += [
        pltpu.VMEM(grid_lat.shape, BF16),
        pltpu.VMEM(mesh_lat.shape, BF16),
        pltpu.VMEM(args[10].shape, BF16),
        pltpu.VMEM(args[11].shape, BF16),
        pltpu.VMEM(args[12].shape, BF16),
        pltpu.VMEM(args[13].shape, BF16),
        pltpu.VMEM(message, BF16),
        pltpu.VMEM(message, BF16),
        pltpu.VMEM(message, BF16),
        pltpu.VMEM((rows, width), F32),
        pltpu.VMEM((edges, 2 * own2 + 2 * RIM), BF16),
        pltpu.VMEM((own2, edges), BF16),
        pltpu.VMEM((own2 + 2 * RIM, width), BF16),
        pltpu.VMEM((2 * own2 + 2 * RIM, width), BF16),
        pltpu.VMEM((edges, width), F32),
        pltpu.VMEM((edges, width), BF16),
        pltpu.VMEM((rows, width), BF16),
        pltpu.VMEM((rows, width), BF16),
        pltpu.VMEM((rows, width), BF16),
        pltpu.VMEM((rows, width), BF16),
        dma((17,)),
        dma((owners,)),
        dma((owners,)),
        dma((owners,)),
        dma((owners,)),
        dma((2,)),
        dma((2,)),
        dma((PARTS,)),
        dma((PARTS,)),
        dma((PARTS,)),
        dma((PARTS,)),
        dma((1,)),
        dma((1,)),
    ]
    shapes = [jax.ShapeDtypeStruct((rows, width), BF16)] * 2
    outs = pl.pallas_call(
        functools.partial(kernel, owners, feats),
        out_shape=shapes,
        in_specs=[hbm] * 16,
        out_specs=[hbm, hbm],
        scratch_shapes=scratch,
        compiler_params=pltpu.CompilerParams(
            collective_id=0, has_side_effects=True, vmem_limit_bytes=LIMIT
        ),
    )(*args)
    return pl.pallas_call(
        finish,
        out_shape=shapes,
        in_specs=[hbm, hbm],
        out_specs=[hbm, hbm],
        scratch_shapes=[pltpu.VMEM((rows, width), BF16)] * 2 + [dma((4,))],
    )(*outs)


def solution(mesh):
    split = P(("groups", "dom", "feat", "sub"), None)
    feats = mesh.shape["feat"]
    owners = mesh.shape["dom"] * feats
    return jax.shard_map(
        functools.partial(on_device, owners, feats),
        mesh=mesh,
        in_specs=(split,) * 10 + (P(),) * 6,
        out_specs=(split, split),
        check_vma=False,
    )
```
